256 devices in a mesh: wide: 32 (over x, y, core), narrow: 8 (over z).
Axes of the slice: x: 4, y: 4, z: 8, core: 2. Of those that a mesh axis runs over, the one named last changes fastest.
Arguments:
- hidden: bfloat16 [4096, 4096], P('wide', 'narrow'), may hold values from -6 to 6
- head_weight: bfloat16 [131072, 4096], P('wide', 'narrow'), may hold values from -0.25 to 0.25
- lse: float32 [4096], replicated, may hold values from 12 to 14
- targets: int32 [4096], replicated, may hold values from 0 to 131071
- loss_weight: float32 [4096], replicated, may hold values from 16 to 48
- block_tiles: int32 [32, 32, 4], P(None, 'wide'), may hold values from 0 to 31, as said below
- block_counts: int32 [32, 32], P(None, 'wide'), may hold values from 0 to 4, as said below
- gate_pre: bfloat16 [4096, 7168], P('wide', 'narrow'), may hold values from -6 to 6
- up_pre: bfloat16 [4096, 7168], P('wide', 'narrow'), may hold values from -6 to 6
- down_weight: bfloat16 [7168, 4096], P('narrow'), may hold values from -0.0625 to 0.0625
Outputs:
- head_grad: bfloat16 [4096, 4096], P('wide', 'narrow')
- gate_grad: bfloat16 [4096, 7168], P('wide', 'narrow')
- up_grad: bfloat16 [4096, 7168], P('wide', 'narrow')
The draws below stay inside these ranges and needn't reach their ends.
Inputs may be any that keep to these rules, and one draw needn't show every extreme that they name: The first block_counts[b, s] entries of block_tiles[b, s] are distinct; the other entries are ignored. `block_counts`: some row block has 4 active tiles in some shard; one shard has exactly 64 active tiles over all row blocks, and no shard has more.
All inputs are finite; a program needn't handle non-finite values.
Results may differ from the reference program's by a relative error of at most 0.0035.
The reference program's roundings to bfloat16 on the way (of `cell_probs`) count: a program that leaves them out, or rounds other values in their place, can miss the bound.
Values may be sent and summed in bfloat16 or wider, within the bound.
A program may use at most 128 MiB of HBM per device.

```python
import math
import jax
import jax.numpy as jnp
import numpy as np
from jax import lax

D = 4096
FF = 7168
VOC_DEV = 4096
TILE = 128
MAXT = 4
ROWS = 4096
SHARDS = 32
VOCAB = 131072
TILES_SHARD = 32
BLOCKS = 32


def tile_plan(key):
    planned = jax.random.fold_in(key, 4099)
    hot_key, rank_key, spare_key, tile_key = jax.random.split(planned, 4)
    hot_shard = jax.random.randint(hot_key, (), 0, SHARDS)
    ranking = jax.random.permutation(rank_key, BLOCKS)
    heavy_rows = jnp.where(ranking < BLOCKS // 2, MAXT, 0)
    spare = jax.random.randint(spare_key, (BLOCKS, SHARDS), 0, MAXT // 2 + 1)
    is_hot = jnp.arange(SHARDS) == hot_shard
    counts = jnp.where(is_hot[None, :], heavy_rows[:, None], spare).astype(jnp.int32)
    tile_keys = jax.random.split(tile_key, BLOCKS * SHARDS)
    chosen = jax.vmap(lambda one_key: jax.random.permutation(one_key, TILES_SHARD)[:MAXT])(tile_keys)
    return (counts, chosen.reshape(BLOCKS, SHARDS, MAXT).astype(jnp.int32))


def draw_block_counts(key, part):
    return tile_plan(key)[0]


def draw_block_tiles(key, part):
    return tile_plan(key)[1]


def draw_hidden(key, part):
    return jax.random.truncated_normal(key, -6.0, 6.0, (ROWS, D), jnp.float32).astype(jnp.bfloat16)


def plant(entries, key, low, high):
    index_at = [jax.random.randint(jax.random.fold_in(key, axis), (), 0, length) for axis, length in enumerate(entries.shape)]
    main_axis = entries.shape.index(max(entries.shape))
    neighbour = index_at[:main_axis] + [(index_at[main_axis] + 1) % entries.shape[main_axis]] + index_at[main_axis + 1:]
    return entries.at[tuple(index_at)].set(low).at[tuple(neighbour)].set(high)


def steps_of(key, extent, cuts, least, largest):
    level = 1.0
    for position, shards_of in cuts:
        steps = jax.random.uniform(jax.random.fold_in(jax.random.fold_in(key, 6), position), (shards_of,), jnp.float32, least / len(cuts), largest / len(cuts))
        level = level * jnp.repeat(jnp.exp(steps), extent[position] // shards_of).reshape((-1,) + (1,) * (len(extent) - 1 - position))
    return level


def skewed_wide(stream_key, shape, count, skew):
    portions = [min(1 << octave, count + 1 - (1 << octave)) * (1 << 20) // math.isqrt((1 << octave) ** skew) + 1 for octave in range((count + 1).bit_length()) if 1 << octave <= count]
    width = 1 + sum(portions) // (1 << 30)
    table = np.cumsum(np.array([max(1, weight // width) for weight in portions]))
    lot = jax.random.randint(jax.random.fold_in(stream_key, 1), shape, 0, int(table[len(portions) - 1]))
    start = jnp.left_shift(1, jnp.searchsorted(jnp.asarray(table, jnp.int32), lot, side="right").astype(jnp.int32))
    rank = start - 1 + jax.random.randint(jax.random.fold_in(stream_key, 4), shape, 0, 1 << 30) % jnp.minimum(start, count + 1 - start)
    return jax.random.permutation(jax.random.fold_in(stream_key, 2), count)[rank].astype(jnp.int32)


def gaussian(stream_key, extent, width, bound, shards=(), kind=jnp.bfloat16):
    level = steps_of(stream_key, extent, shards, -0.22, 0.18) if shards else 1.0
    entries = jax.random.normal(stream_key, extent, jnp.float32) * width * level
    return jnp.minimum(jnp.maximum(entries, -bound), bound).astype(kind)


def setup_inputs(seed: int = 0) -> dict:
    streams_of = jax.random.split(jax.random.key(seed), 11)
    hidden = draw_hidden(jax.random.fold_in(streams_of[10], 71), 0)
    head_weight = gaussian(streams_of[1], (VOCAB, D), (D // 9) ** -0.5, 0.25, ((0, 32), (1, 8)))
    lse = jnp.clip(jax.random.uniform(streams_of[2], (ROWS,), jnp.float32, 12.0, 14.0), 12.0, 14.0)
    targets = plant(skewed_wide(streams_of[3], (ROWS,), VOCAB, 2), jax.random.fold_in(streams_of[3], 3), 0, VOCAB - 1).astype(jnp.int32)
    loss_weight = jnp.clip(jax.random.uniform(streams_of[4], (ROWS,), jnp.float32, 16.0, 48.0), 16.0, 48.0)
    block_tiles = draw_block_tiles(jax.random.fold_in(streams_of[10], 71), 0)
    block_counts = draw_block_counts(jax.random.fold_in(streams_of[10], 71), 0)
    gate_pre = gaussian(streams_of[7], (ROWS, FF), 1.5, 6.0, ((0, 32), (1, 8)))
    up_pre = gaussian(streams_of[8], (ROWS, FF), 1.0, 6.0, ((0, 32), (1, 8)))
    down_weight = gaussian(streams_of[9], (FF, D), FF ** -0.5, 0.0625, ((0, 8),))
    return {"hidden": hidden, "head_weight": head_weight, "lse": lse, "targets": targets, "loss_weight": loss_weight, "block_tiles": block_tiles, "block_counts": block_counts, "gate_pre": gate_pre, "up_pre": up_pre, "down_weight": down_weight}


def reference(hidden, head_weight, lse, targets, loss_weight, block_tiles, block_counts, gate_pre, up_pre, down_weight):
    blocks = ROWS // TILE
    shard_start = jnp.arange(SHARDS, dtype=jnp.int32)[:, None] * VOC_DEV
    within = jnp.arange(TILE, dtype=jnp.int32)
    slot_ids = jnp.arange(MAXT, dtype=jnp.int32)

    def one_block(items):
        row_block, lse_rows, scale_rows, tiles_row, counts_row, target_row = items
        first_cols = shard_start + tiles_row.astype(jnp.int32) * TILE
        columns = first_cols[:, :, None] + within[None, None, :]
        picked = jnp.take(head_weight, columns.reshape(-1).astype(jnp.int32), axis=0)
        picked = picked.astype(jnp.float32).reshape(SHARDS, MAXT, TILE, D)
        logits = jnp.einsum("rd,smcd->smrc", row_block.astype(jnp.float32), picked)
        scaled = jnp.exp(logits - lse_rows[None, None, :, None]) * scale_rows[None, None, :, None]
        live_slots = slot_ids[None, :] < counts_row[:, None]
        cell_probs = jnp.where(live_slots[:, :, None, None], scaled, jnp.zeros_like(scaled)).astype(jnp.bfloat16)
        cell_probs = lax.optimization_barrier(cell_probs).astype(jnp.float32)
        softmax_part = jnp.einsum("smrc,smcd->rd", cell_probs, picked)
        target_rows = jnp.take(head_weight, target_row.astype(jnp.int32), axis=0).astype(jnp.float32)
        return softmax_part - scale_rows[:, None] * target_rows

    grads = lax.map(one_block, (hidden.reshape(blocks, TILE, D), lse.reshape(blocks, TILE),
                                loss_weight.reshape(blocks, TILE), block_tiles, block_counts,
                                targets.reshape(blocks, TILE)))
    head_grad = grads.reshape(ROWS, D).astype(jnp.bfloat16)
    unit_grad = jnp.dot(head_grad, down_weight.T, preferred_element_type=jnp.float32)
    gate_value = gate_pre.astype(jnp.float32)
    up_value = up_pre.astype(jnp.float32)
    gate_sig = jax.nn.sigmoid(gate_value)
    up_grad = (unit_grad * gate_value * gate_sig).astype(jnp.bfloat16)
    gate_grad = (unit_grad * up_value * gate_sig * (1.0 + gate_value * (1.0 - gate_sig))).astype(jnp.bfloat16)
    return (head_grad, gate_grad, up_grad)
```

```python
import jax
import jax.numpy as jnp
from jax import lax
from jax.experimental import pallas as pl
from jax.experimental.pallas import tpu as pltpu
from jax.sharding import PartitionSpec as P

MESH = pl.DeviceIdType.MESH
F32 = jnp.float32
BF16 = jnp.bfloat16
I16 = jnp.int16
I32 = jnp.int32
TILE = 128
SLOTS = 64
BLOCKS = 32
MAXT = 4
FEAT = 512
HU = 896
VT = 32
Z = 8
HALF = 4
UNIT = HALF * TILE + 16


def scale_exponent(top):
    return jnp.clip(jnp.ceil(jnp.log2(top)), -100.0, 127.0)


def code(value, exponent):
    return jnp.round(value * jnp.exp2(14.875 - exponent)).astype(I32).astype(I16)


def factor_of(exponent16):
    return jnp.exp2(exponent16.astype(I32).astype(F32) - 14.875)


def to_f32(coded):
    return coded.astype(I32).astype(F32)


def body(
    hidden,
    weight,
    lse,
    targets,
    scale,
    tiles,
    counts,
    gate,
    up,
    down,
    hg_out,
    gg_out,
    ug_out,
    hid,
    w,
    dw,
    lp,
    probs,
    acc_own,
    acc_sib,
    sib,
    zs,
    zr,
    s1,
    r1,
    s2,
    r2,
    hg,
    unit,
    lse_rows,
    scale_rows,
    pos,
    slot_block,
    slot_tile,
    local_sem,
    hs_sem,
    hr_sem,
    zs_sem,
    zr_sem,
    ps_sem,
    pr_sem,
    bs_sem,
    br_sem,
    s1s_sem,
    s1r_sem,
    s2s_sem,
    s2r_sem,
    gs_sem,
    gr_sem,
):
    me = lax.axis_index("wide")
    z = lax.axis_index("narrow")
    x = me // 8
    y = (me // 2) % 4
    c = me % 2

    def placed(i, j, core):
        xi = i * (1 - core) + j * core
        yi = j * (1 - core) + i * core
        return ((x + xi) % 4) * 8 + ((y + yi) % 4) * 2 + core

    def at(i, j):
        return placed(i, j, c)

    sibling = (x * 8 + y * 2 + 1 - c, z)
    right = (me, (z + 1) % Z)
    left = (me, (z + Z - 1) % Z)

    def remote(src, dst, send, recv, device):
        return pltpu.make_async_remote_copy(
            src_ref=src, dst_ref=dst, send_sem=send, recv_sem=recv, device_id=device, device_id_type=MESH
        )

    own_copy = pltpu.make_async_copy(hidden, hid.at[me], local_sem.at[0])
    own_copy.start()
    w_copy = pltpu.make_async_copy(weight, w, local_sem.at[1])
    w_copy.start()
    dw_copy = pltpu.make_async_copy(down, dw, local_sem.at[2])
    dw_copy.start()

    barrier = pltpu.get_barrier_semaphore()
    peers = [sibling, right, left]
    peers += [(at(i, 0), z) for i in (1, 2, 3)] + [(at(0, j), z) for j in (1, 2, 3)]
    for peer in peers:
        pl.semaphore_signal(barrier, inc=1, device_id=peer, device_id_type=MESH)
    pl.semaphore_wait(barrier, len(peers))

    sends = []

    def go(copy):
        copy.start()
        sends.append(copy)

    def block_send(src, b, k, device):
        go(remote(src, hid.at[b], hs_sem.at[k], hr_sem.at[b], device))

    def block_wait(b):
        remote(hid.at[b], hid.at[b], hs_sem.at[0], hr_sem.at[b], sibling).wait_recv()

    for i in (1, 3, 2):
        block_send(hidden, me, i - 1, (at(i, 0), z))
    for j in (1, 3, 2):
        block_send(hidden, me, 2 + j, (at(0, j), z))
    block_send(hidden, me, 15, sibling)

    def prefix(b, run):
        pos[b] = run
        return run + counts[b, 0]

    pos[BLOCKS] = lax.fori_loop(0, BLOCKS, prefix, jnp.int32(0))

    def fill(s, carry):
        before = jnp.int32(0)
        for b in range(BLOCKS):
            before = before + jnp.clip(s + 1 - pos[b + 1], 0, 1)
        b = jnp.minimum(before, BLOCKS - 1)
        j = jnp.clip(s - pos[b], 0, MAXT - 1)
        slot_block[s] = b
        slot_tile[s] = jnp.clip(tiles[b, 0, j], 0, VT - 1)
        return carry

    lane = lax.broadcasted_iota(I32, (TILE, TILE), 1)
    first = me * (VT * TILE)

    def target_block(acc, k, b):
        ids = jnp.broadcast_to(targets[pl.ds(b, 1), :] - first, (TILE, TILE)).astype(F32).T.astype(I32)
        total = jnp.zeros((TILE, FEAT), F32)
        for v in range(0, VT, 4):
            hot = jnp.concatenate(
                [jnp.where(ids == lane + (v + u) * TILE, 1.0, 0.0).astype(BF16) for u in range(4)], axis=1
            )
            total = total + jnp.dot(hot, w[v : v + 4].reshape(4 * TILE, FEAT), preferred_element_type=F32)
        weights = jnp.broadcast_to(scale[pl.ds(b, 1), :], (TILE, TILE)).T
        for n in range(FEAT // TILE):
            part = slice(n * TILE, (n + 1) * TILE)
            acc[k, :, part] = -weights * total[:, part]

    def target_blocks(lo, hi):
        def pair(k, carry):
            target_block(acc_sib, k, placed(k // 4, k % 4, 1 - c))
            target_block(acc_own, k, placed(k // 4, k % 4, c))
            return carry

        lax.fori_loop(lo // 2, hi // 2, pair, 0)

    lax.fori_loop(0, SLOTS, fill, 0)
    for b in range(BLOCKS):
        lse_rows[b] = jnp.broadcast_to(lse[b : b + 1, :], (8, TILE))
        scale_rows[b] = jnp.broadcast_to(scale[b : b + 1, :], (8, TILE))
    probs[SLOTS] = jnp.zeros((TILE, TILE), BF16)
    w_copy.wait()
    for i in (1, 3, 2):
        b = at(i, 0)
        block_wait(b)
        for j in (1, 3, 2):
            block_send(hid.at[b], b, 2 + i * 3 + j, (at(0, j), z))
        block_send(hid.at[b], b, 15 + i, sibling)
        target_blocks((i - 1) * 2, i * 2)
    for j in (1, 3, 2):
        for i in (0, 1, 3, 2):
            b = at(i, j)
            block_wait(b)
            block_send(hid.at[b], b, 15 + j * 4 + i, sibling)
    own_copy.wait()
    for k in range(16):
        block_wait(2 * k + 1 - c)

    def logits(chunk):
        def slot(i, carry):
            s = chunk * 8 + i
            rows = hid[slot_block[s]]
            entries = w[slot_tile[s]]
            lp[s] = lax.dot_general(entries, rows, (((1,), (1,)), ((), ())), preferred_element_type=F32)
            return carry

        lax.fori_loop(0, 8, slot, 0, unroll=4)

    row16 = lax.broadcasted_iota(I32, (16, TILE), 0) // 4

    def unit_code(k, chunk, half, arrived):
        base = chunk * 8 + half * HALF
        if arrived is not None:
            factors = factor_of(zr[arrived, HALF * TILE : UNIT, :])

        def slot(i, exps):
            value = lp[base + i]
            if arrived is not None:
                factor = jnp.max(jnp.where(row16 == i, factors, 0.0), axis=0, keepdims=True)
                value = value + to_f32(zr[arrived, pl.ds(pl.multiple_of(i * TILE, TILE), TILE), :]) * factor
            e = scale_exponent(jnp.max(jnp.abs(value), axis=0, keepdims=True))
            zs[k, pl.ds(pl.multiple_of(i * TILE, TILE), TILE), :] = code(value, e)
            return jnp.where(row16 == i, e, exps)

        exps = lax.fori_loop(0, HALF, slot, jnp.zeros((16, TILE), F32))
        zs[k, HALF * TILE : UNIT, :] = exps.astype(I32).astype(I16)

    def unit_index(direction, step, half):
        return direction * 8 + step * 2 + half

    def unit_send(direction, step, half):
        k = unit_index(direction, step, half)
        go(remote(zs.at[k], zr.at[k], zs_sem.at[k], zr_sem.at[k], (right, left)[direction]))

    def unit_wait(direction, step, half):
        k = unit_index(direction, step, half)
        remote(zs.at[k], zr.at[k], zs_sem.at[k], zr_sem.at[k], right).wait_recv()
        return k

    def away(direction, distance):
        return (z + (distance if direction == 0 else Z - distance)) % Z

    logits(away(0, 4))
    for direction in (0, 1):
        unit_code(unit_index(direction, 0, direction), away(0, 4), direction, None)
        unit_send(direction, 0, direction)
    for direction in (0, 1):
        logits(away(direction, 3))
        half = 1 - direction
        unit_code(unit_index(direction, 1, half), away(direction, 3), half, None)
        unit_send(direction, 1, half)
    logits(away(0, 2))
    logits(away(1, 2))
    for step in (1, 2, 3):
        for half in (0, 1):
            for direction in (0, 1):
                h = half if direction == 0 else 1 - half
                if step == 1 and h != direction:
                    continue
                k = unit_wait(direction, step - 1, h)
                unit_code(unit_index(direction, step, h), away(direction, 4 - step), h, k)
                unit_send(direction, step, h)
        if step == 1:
            logits(away(0, 1))
            logits(away(1, 1))
            logits(z)
        target_blocks(4 + step * 2, 6 + step * 2)

    def part_refs(t, chunk, half):
        return probs.at[pl.ds(chunk * 8 + half * HALF, HALF)]

    def p_send(direction, step, half):
        k = unit_index(direction, step, half)
        part = part_refs(step, away(1 - direction, step), half)
        go(remote(part, part, ps_sem.at[k], pr_sem.at[k], (right, left)[direction]))

    def p_wait(direction, step, half):
        k = unit_index(direction, step, half)
        part = part_refs(step, away(1 - direction, step + 1), half)
        remote(part, part, ps_sem.at[k], pr_sem.at[k], right).wait_recv()

    for half in (0, 1):
        ka = unit_wait(0, 3, half)
        kb = unit_wait(1, 3, half)
        fa = factor_of(zr[ka, HALF * TILE : UNIT, :])
        fb = factor_of(zr[kb, HALF * TILE : UNIT, :])

        def prob_slot(i, carry, ka=ka, kb=kb, fa=fa, fb=fb, half=half):
            s = z * 8 + half * HALF + i
            part = pl.ds(pl.multiple_of(i * TILE, TILE), TILE)
            factor_a = jnp.max(jnp.where(row16 == i, fa, 0.0), axis=0, keepdims=True)
            factor_b = jnp.max(jnp.where(row16 == i, fb, 0.0), axis=0, keepdims=True)
            value = lp[s] + to_f32(zr[ka, part, :]) * factor_a + to_f32(zr[kb, part, :]) * factor_b
            b = slot_block[s]
            value = jnp.exp(value - lse_rows[b][0:1, :]) * scale_rows[b][0:1, :]
            probs[s] = value.T.astype(BF16)
            return carry

        lax.fori_loop(0, HALF, prob_slot, 0)
        for direction in (0, 1):
            p_send(direction, 0, half)
    target_blocks(12, 16)
    for step in (1, 2, 3):
        for half in (0, 1):
            for direction in (0, 1):
                h = half if direction == 0 else 1 - half
                p_wait(direction, step - 1, h)
                if step < 3 or h == direction:
                    p_send(direction, step, h)
        target_blocks(12 + step * 4, 16 + step * 4)
    target_blocks(28, 32)
    for direction in (0, 1):
        p_wait(direction, 3, direction)

    def contribution(acc, k, b):
        taken, entries = [], []
        for j in range(MAXT):
            live = jnp.clip(counts[b, 0] - j, 0, 1)
            taken.append(probs[jnp.clip(live * (pos[b] + j) + (1 - live) * SLOTS, 0, SLOTS)])
            entries.append(w[jnp.clip(tiles[b, 0, j], 0, VT - 1)])
        acc[k] = acc[k] + jnp.dot(
            jnp.concatenate(taken, axis=1), jnp.concatenate(entries, axis=0), preferred_element_type=F32
        )

    def sib_copy(k):
        return remote(acc_sib.at[k], sib.at[k], bs_sem.at[k], br_sem.at[k], sibling)

    def for_sibling(k, carry):
        contribution(acc_sib, k, placed(k // 4, k % 4, 1 - c))
        return carry

    lax.fori_loop(0, 16, for_sibling, 0)
    for k in range(16):
        go(sib_copy(k))

    def for_own(k, carry):
        contribution(acc_own, k, placed(k // 4, k % 4, c))
        return carry

    lax.fori_loop(0, 16, for_own, 0)
    for k in range(16):
        sib_copy(k).wait_recv()

    def block_code(dst, k, value):
        e = scale_exponent(jnp.max(jnp.abs(value), axis=0, keepdims=True))
        dst[k, 0:TILE, :] = code(value, e)
        dst[k, TILE : TILE + 16, :] = jnp.broadcast_to(e, (16, FEAT)).astype(I32).astype(I16)

    def block_decode(src, k):
        factor = factor_of(src[k, TILE : TILE + 16, :])[0:1, :]
        return to_f32(src[k, 0:TILE, :]) * factor

    def first_copy(i, j):
        k = (j - 1) * 4 + i
        return remote(s1.at[k], r1.at[k], s1s_sem.at[k], s1r_sem.at[k], (at(0, j), z))

    def second_copy(i):
        return remote(s2.at[i - 1], r2.at[i - 1], s2s_sem.at[i - 1], s2r_sem.at[i - 1], (at(i, 0), z))

    for i in (1, 3, 2, 0):
        for j in (1, 3, 2):
            k = i * 4 + j
            block_code(s1, (j - 1) * 4 + i, acc_own[k] + sib[k])
            go(first_copy(i, j))
    for i in (1, 3, 2, 0):
        k = i * 4
        value = acc_own[k] + sib[k]
        for j in (1, 3, 2):
            first_copy(i, j).wait_recv()
            value = value + block_decode(r1, (j - 1) * 4 + i)
        if i:
            block_code(s2, i - 1, value)
            go(second_copy(i))
    for i in (1, 3, 2):
        second_copy(i).wait_recv()
        value = value + block_decode(r2, i - 1)
    own = value.astype(BF16)
    hg[7] = own
    hg_out[...] = own

    def g_place(direction, step):
        return 7 if step < 0 else min(step * 2 + direction, 6)

    def g_copy(direction, step, half):
        k = unit_index(direction, step, half)
        rows = pl.ds(half * 64, 64)
        return remote(
            hg.at[g_place(direction, step - 1), rows],
            hg.at[g_place(direction, step), rows],
            gs_sem.at[k],
            gr_sem.at[k],
            (right, left)[direction],
        )

    def unit_part(place, chunk):
        cols = dw[:, pl.ds(pl.multiple_of(chunk * FEAT, FEAT), FEAT)]
        return lax.dot_general(hg[place], cols, (((1,), (1,)), ((), ())), preferred_element_type=F32)

    for half in (0, 1):
        for direction in (0, 1):
            go(g_copy(direction, 0, half))
    dw_copy.wait()
    unit[...] = unit_part(7, z)
    for step in (1, 2, 3):
        for half in (0, 1):
            for direction in (0, 1):
                h = half if direction == 0 else 1 - half
                g_copy(direction, step - 1, h).wait_recv()
                if step < 3 or h == direction:
                    go(g_copy(direction, step, h))
        for direction in (0, 1):
            unit[...] += unit_part(g_place(direction, step - 1), away(1 - direction, step))
    for direction in (0, 1):
        g_copy(direction, 3, direction).wait_recv()
    unit[...] += unit_part(6, away(0, 4))

    for k in range(HU // TILE):
        part = slice(k * TILE, (k + 1) * TILE)
        grad = unit[:, part]
        g = gate[:, part].astype(F32)
        u = up[:, part].astype(F32)
        sig = 1.0 / (1.0 + jnp.exp(-g))
        ug_out[:, part] = (grad * g * sig).astype(BF16)
        gg_out[:, part] = (grad * u * sig * (1.0 + g * (1.0 - sig))).astype(BF16)

    for copy in sends:
        copy.wait_send()


def on_device(hidden, head_weight, lse, targets, loss_weight, block_tiles, block_counts, gate_pre, up_pre, down_weight):
    vmem = pl.BlockSpec(memory_space=pltpu.VMEM)
    smem = pl.BlockSpec(memory_space=pltpu.SMEM)
    hbm = pl.BlockSpec(memory_space=pl.ANY)
    dma = pltpu.SemaphoreType.DMA
    return pl.pallas_call(
        body,
        out_shape=(
            jax.ShapeDtypeStruct((TILE, FEAT), BF16),
            jax.ShapeDtypeStruct((TILE, HU), BF16),
            jax.ShapeDtypeStruct((TILE, HU), BF16),
        ),
        in_specs=[hbm, hbm, vmem, vmem, vmem, smem, smem, vmem, vmem, hbm],
        out_specs=(vmem, vmem, vmem),
        scratch_shapes=[
            pltpu.VMEM((BLOCKS, TILE, FEAT), BF16),
            pltpu.VMEM((VT, TILE, FEAT), BF16),
            pltpu.VMEM((HU, Z * FEAT), BF16),
            pltpu.VMEM((SLOTS, TILE, TILE), F32),
            pltpu.VMEM((SLOTS + 1, TILE, TILE), BF16),
            pltpu.VMEM((16, TILE, FEAT), F32),
            pltpu.VMEM((16, TILE, FEAT), F32),
            pltpu.VMEM((16, TILE, FEAT), F32),
            pltpu.VMEM((16, UNIT, TILE), I16),
            pltpu.VMEM((16, UNIT, TILE), I16),
            pltpu.VMEM((12, TILE + 16, FEAT), I16),
            pltpu.VMEM((12, TILE + 16, FEAT), I16),
            pltpu.VMEM((3, TILE + 16, FEAT), I16),
            pltpu.VMEM((3, TILE + 16, FEAT), I16),
            pltpu.VMEM((Z, TILE, FEAT), BF16),
            pltpu.VMEM((TILE, HU), F32),
            pltpu.VMEM((BLOCKS, 8, TILE), F32),
            pltpu.VMEM((BLOCKS, 8, TILE), F32),
            pltpu.SMEM((BLOCKS + 1,), I32),
            pltpu.SMEM((SLOTS,), I32),
            pltpu.SMEM((SLOTS,), I32),
            dma((3,)),
            dma((31,)),
            dma((32,)),
            dma((16,)),
            dma((16,)),
            dma((16,)),
            dma((16,)),
            dma((16,)),
            dma((16,)),
            dma((12,)),
            dma((12,)),
            dma((3,)),
            dma((3,)),
            dma((16,)),
            dma((16,)),
        ],
        compiler_params=pltpu.CompilerParams(
            collective_id=0, has_side_effects=True, vmem_limit_bytes=60 * 2**20
        ),
        cost_estimate=pl.CostEstimate(flops=4 * 10**9, bytes_accessed=13 * 10**6, transcendentals=10**6),
    )(
        hidden,
        head_weight.reshape(VT, TILE, FEAT),
        lse.reshape(BLOCKS, TILE),
        targets.reshape(BLOCKS, TILE),
        loss_weight.reshape(BLOCKS, TILE),
        block_tiles,
        block_counts,
        gate_pre,
        up_pre,
        down_weight,
    )


def solution(mesh):
    in_specs = (
        P("wide", "narrow"),
        P("wide", "narrow"),
        P(),
        P(),
        P(),
        P(None, "wide", None),
        P(None, "wide"),
        P("wide", "narrow"),
        P("wide", "narrow"),
        P("narrow", None),
    )
    out_specs = (P("wide", "narrow"), P("wide", "narrow"), P("wide", "narrow"))
    return jax.shard_map(on_device, mesh=mesh, in_specs=in_specs, out_specs=out_specs, check_vma=False)
```

```python
import jax
import jax.numpy as jnp
from jax import lax
from jax.experimental import pallas as pl
from jax.experimental.pallas import tpu as pltpu
from jax.sharding import PartitionSpec as P

MESH = pl.DeviceIdType.MESH
F32 = jnp.float32
BF16 = jnp.bfloat16
I16 = jnp.int16
I32 = jnp.int32
TILE = 128
SLOTS = 64
BLOCKS = 32
MAXT = 4
FEAT = 512
HU = 896
VT = 32
Z = 8
HALF = 4
UNIT = HALF * TILE + 16


def scale_exponent(top):
    return jnp.clip(jnp.ceil(jnp.log2(top)), -100.0, 127.0)


def code(value, exponent):
    return jnp.round(value * jnp.exp2(14.875 - exponent)).astype(I32).astype(I16)


def factor_of(exponent16):
    return jnp.exp2(exponent16.astype(I32).astype(F32) - 14.875)


def to_f32(coded):
    return coded.astype(I32).astype(F32)


def body(
    hidden,
    weight,
    lse,
    targets,
    scale,
    tiles_in,
    counts_in,
    gate,
    up,
    down,
    hg_out,
    gg_out,
    ug_out,
    hid,
    w,
    dw,
    lp,
    probs,
    acc_own,
    acc_sib,
    sib,
    zs,
    zr,
    s1,
    r1,
    s2,
    r2,
    hg,
    unit,
    lse_rows,
    scale_rows,
    tiles,
    counts,
    pos,
    slot_block,
    slot_tile,
    local_sem,
    hs_sem,
    hr_sem,
    zs_sem,
    zr_sem,
    ps_sem,
    pr_sem,
    bs_sem,
    br_sem,
    s1s_sem,
    s1r_sem,
    s2s_sem,
    s2r_sem,
    gs_sem,
    gr_sem,
):
    me = lax.axis_index("wide")
    z = lax.axis_index("narrow")
    x = me // 8
    y = (me // 2) % 4
    c = me % 2

    def placed(i, j, core):
        xi = i * (1 - core) + j * core
        yi = j * (1 - core) + i * core
        return ((x + xi) % 4) * 8 + ((y + yi) % 4) * 2 + core

    def at(i, j):
        return placed(i, j, c)

    sibling = (x * 8 + y * 2 + 1 - c, z)
    right = (me, (z + 1) % Z)
    left = (me, (z + Z - 1) % Z)

    def remote(src, dst, send, recv, device):
        return pltpu.make_async_remote_copy(
            src_ref=src, dst_ref=dst, send_sem=send, recv_sem=recv, device_id=device, device_id_type=MESH
        )

    own_copy = pltpu.make_async_copy(hidden, hid.at[me], local_sem.at[0])
    own_copy.start()
    w_copy = pltpu.make_async_copy(weight, w, local_sem.at[1])
    w_copy.start()
    dw_copy = pltpu.make_async_copy(down, dw, local_sem.at[2])
    dw_copy.start()
    tiles_copy = pltpu.make_async_copy(tiles_in, tiles, local_sem.at[3])
    tiles_copy.start()
    counts_copy = pltpu.make_async_copy(counts_in, counts, local_sem.at[4])
    counts_copy.start()

    barrier = pltpu.get_barrier_semaphore()
    peers = [sibling, right, left]
    peers += [(at(i, 0), z) for i in (1, 2, 3)] + [(at(0, j), z) for j in (1, 2, 3)]
    for peer in peers:
        pl.semaphore_signal(barrier, inc=1, device_id=peer, device_id_type=MESH)
    pl.semaphore_wait(barrier, len(peers))

    sends = []

    def go(copy):
        copy.start()
        sends.append(copy)

    def block_send(src, b, k, device):
        go(remote(src, hid.at[b], hs_sem.at[k], hr_sem.at[b], device))

    def block_wait(b):
        remote(hid.at[b], hid.at[b], hs_sem.at[0], hr_sem.at[b], sibling).wait_recv()

    for i in (1, 3, 2):
        block_send(hidden, me, i - 1, (at(i, 0), z))
    for j in (1, 3, 2):
        block_send(hidden, me, 2 + j, (at(0, j), z))
    block_send(hidden, me, 15, sibling)

    def prefix(b, run):
        pos[b] = run
        return run + counts[b, 0]

    def fill(s, carry):
        before = jnp.int32(0)
        for b in range(BLOCKS):
            before = before + jnp.clip(s + 1 - pos[b + 1], 0, 1)
        b = jnp.minimum(before, BLOCKS - 1)
        j = jnp.clip(s - pos[b], 0, MAXT - 1)
        slot_block[s] = b
        slot_tile[s] = jnp.clip(tiles[b, 0, j], 0, VT - 1)
        return carry

    lane = lax.broadcasted_iota(I32, (TILE, TILE), 1)
    first = me * (VT * TILE)

    def target_block(acc, k, b):
        ids = jnp.broadcast_to(targets[pl.ds(b, 1), :] - first, (TILE, TILE)).astype(F32).T.astype(I32)
        total = jnp.zeros((TILE, FEAT), F32)
        for v in range(0, VT, 4):
            hot = jnp.concatenate(
                [jnp.where(ids == lane + (v + u) * TILE, 1.0, 0.0).astype(BF16) for u in range(4)], axis=1
            )
            total = total + jnp.dot(hot, w[v : v + 4].reshape(4 * TILE, FEAT), preferred_element_type=F32)
        weights = jnp.broadcast_to(scale[pl.ds(b, 1), :], (TILE, TILE)).T
        for n in range(FEAT // TILE):
            part = slice(n * TILE, (n + 1) * TILE)
            acc[k, :, part] = -weights * total[:, part]

    def target_blocks(lo, hi):
        def pair(k, carry):
            target_block(acc_sib, k, placed(k // 4, k % 4, 1 - c))
            target_block(acc_own, k, placed(k // 4, k % 4, c))
            return carry

        lax.fori_loop(lo // 2, hi // 2, pair, 0)

    for i in (1, 3, 2):
        b = at(i, 0)
        block_wait(b)
        for j in (1, 3, 2):
            block_send(hid.at[b], b, 2 + i * 3 + j, (at(0, j), z))
        block_send(hid.at[b], b, 15 + i, sibling)
    tiles_copy.wait()
    counts_copy.wait()
    pos[BLOCKS] = lax.fori_loop(0, BLOCKS, prefix, jnp.int32(0))
    lax.fori_loop(0, SLOTS, fill, 0)
    for b in range(BLOCKS):
        lse_rows[b] = jnp.broadcast_to(lse[b : b + 1, :], (8, TILE))
        scale_rows[b] = jnp.broadcast_to(scale[b : b + 1, :], (8, TILE))
    probs[SLOTS] = jnp.zeros((TILE, TILE), BF16)
    w_copy.wait()
    target_blocks(0, 6)
    for j in (1, 3, 2):
        for i in (0, 1, 3, 2):
            b = at(i, j)
            block_wait(b)
            block_send(hid.at[b], b, 15 + j * 4 + i, sibling)
    own_copy.wait()
    for k in range(16):
        block_wait(2 * k + 1 - c)

    def logits(chunk):
        def slot(i, carry):
            s = chunk * 8 + i
            rows = hid[slot_block[s]]
            entries = w[slot_tile[s]]
            lp[s] = lax.dot_general(entries, rows, (((1,), (1,)), ((), ())), preferred_element_type=F32)
            return carry

        lax.fori_loop(0, 8, slot, 0, unroll=4)

    row16 = lax.broadcasted_iota(I32, (16, TILE), 0) // 4

    def unit_code(k, chunk, half, arrived):
        base = chunk * 8 + half * HALF
        if arrived is not None:
            factors = factor_of(zr[arrived, HALF * TILE : UNIT, :])

        def slot(i, exps):
            value = lp[base + i]
            if arrived is not None:
                factor = jnp.max(jnp.where(row16 == i, factors, 0.0), axis=0, keepdims=True)
                value = value + to_f32(zr[arrived, pl.ds(pl.multiple_of(i * TILE, TILE), TILE), :]) * factor
            e = scale_exponent(jnp.max(jnp.abs(value), axis=0, keepdims=True))
            zs[k, pl.ds(pl.multiple_of(i * TILE, TILE), TILE), :] = code(value, e)
            return jnp.where(row16 == i, e, exps)

        exps = lax.fori_loop(0, HALF, slot, jnp.zeros((16, TILE), F32))
        zs[k, HALF * TILE : UNIT, :] = exps.astype(I32).astype(I16)

    def unit_index(direction, step, half):
        return direction * 8 + step * 2 + half

    def unit_send(direction, step, half):
        k = unit_index(direction, step, half)
        go(remote(zs.at[k], zr.at[k], zs_sem.at[k], zr_sem.at[k], (right, left)[direction]))

    def unit_wait(direction, step, half):
        k = unit_index(direction, step, half)
        remote(zs.at[k], zr.at[k], zs_sem.at[k], zr_sem.at[k], right).wait_recv()
        return k

    def away(direction, distance):
        return (z + (distance if direction == 0 else Z - distance)) % Z

    logits(away(0, 4))
    for direction in (0, 1):
        unit_code(unit_index(direction, 0, direction), away(0, 4), direction, None)
        unit_send(direction, 0, direction)
    for direction in (0, 1):
        logits(away(direction, 3))
        half = 1 - direction
        unit_code(unit_index(direction, 1, half), away(direction, 3), half, None)
        unit_send(direction, 1, half)
    logits(away(0, 2))
    logits(away(1, 2))
    for step in (1, 2, 3):
        for half in (0, 1):
            for direction in (0, 1):
                h = half if direction == 0 else 1 - half
                if step == 1 and h != direction:
                    continue
                k = unit_wait(direction, step - 1, h)
                unit_code(unit_index(direction, step, h), away(direction, 4 - step), h, k)
                unit_send(direction, step, h)
        if step == 1:
            logits(away(0, 1))
            logits(away(1, 1))
            logits(z)
        target_blocks(4 + step * 2, 6 + step * 2)

    def part_refs(t, chunk, half):
        return probs.at[pl.ds(chunk * 8 + half * HALF, HALF)]

    def p_send(direction, step, half):
        k = unit_index(direction, step, half)
        part = part_refs(step, away(1 - direction, step), half)
        go(remote(part, part, ps_sem.at[k], pr_sem.at[k], (right, left)[direction]))

    def p_wait(direction, step, half):
        k = unit_index(direction, step, half)
        part = part_refs(step, away(1 - direction, step + 1), half)
        remote(part, part, ps_sem.at[k], pr_sem.at[k], right).wait_recv()

    for half in (0, 1):
        ka = unit_wait(0, 3, half)
        kb = unit_wait(1, 3, half)
        fa = factor_of(zr[ka, HALF * TILE : UNIT, :])
        fb = factor_of(zr[kb, HALF * TILE : UNIT, :])

        def prob_slot(i, carry, ka=ka, kb=kb, fa=fa, fb=fb, half=half):
            s = z * 8 + half * HALF + i
            part = pl.ds(pl.multiple_of(i * TILE, TILE), TILE)
            factor_a = jnp.max(jnp.where(row16 == i, fa, 0.0), axis=0, keepdims=True)
            factor_b = jnp.max(jnp.where(row16 == i, fb, 0.0), axis=0, keepdims=True)
            value = lp[s] + to_f32(zr[ka, part, :]) * factor_a + to_f32(zr[kb, part, :]) * factor_b
            b = slot_block[s]
            value = jnp.exp(value - lse_rows[b][0:1, :]) * scale_rows[b][0:1, :]
            probs[s] = value.T.astype(BF16)
            return carry

        lax.fori_loop(0, HALF, prob_slot, 0)
        for direction in (0, 1):
            p_send(direction, 0, half)
    target_blocks(12, 16)
    for step in (1, 2, 3):
        for half in (0, 1):
            for direction in (0, 1):
                h = half if direction == 0 else 1 - half
                p_wait(direction, step - 1, h)
                if step < 3 or h == direction:
                    p_send(direction, step, h)
        target_blocks(12 + step * 4, 16 + step * 4)
    target_blocks(28, 32)
    for direction in (0, 1):
        p_wait(direction, 3, direction)

    def contribution(acc, k, b):
        taken, entries = [], []
        for j in range(MAXT):
            live = jnp.clip(counts[b, 0] - j, 0, 1)
            taken.append(probs[jnp.clip(live * (pos[b] + j) + (1 - live) * SLOTS, 0, SLOTS)])
            entries.append(w[jnp.clip(tiles[b, 0, j], 0, VT - 1)])
        acc[k] = acc[k] + jnp.dot(
            jnp.concatenate(taken, axis=1), jnp.concatenate(entries, axis=0), preferred_element_type=F32
        )

    def sib_copy(k):
        return remote(acc_sib.at[k], sib.at[k], bs_sem.at[k], br_sem.at[k], sibling)

    def group_for_sibling(i):
        def one(k, carry):
            contribution(acc_sib, k, placed(k // 4, k % 4, 1 - c))
            return carry

        lax.fori_loop(i * 4, i * 4 + 4, one, 0)
        for j in range(4):
            go(sib_copy(i * 4 + j))

    def group_own(i):
        def one(k, carry):
            contribution(acc_own, k, placed(k // 4, k % 4, c))
            return carry

        lax.fori_loop(i * 4, i * 4 + 4, one, 0)

    def block_code(dst, k, value):
        e = scale_exponent(jnp.max(jnp.abs(value), axis=0, keepdims=True))
        dst[k, 0:TILE, :] = code(value, e)
        dst[k, TILE : TILE + 16, :] = jnp.broadcast_to(e, (16, FEAT)).astype(I32).astype(I16)

    def block_decode(src, k):
        factor = factor_of(src[k, TILE : TILE + 16, :])[0:1, :]
        return to_f32(src[k, 0:TILE, :]) * factor

    def first_copy(i, j):
        k = (j - 1) * 4 + i
        return remote(s1.at[k], r1.at[k], s1s_sem.at[k], s1r_sem.at[k], (at(0, j), z))

    def second_copy(i):
        return remote(s2.at[i - 1], r2.at[i - 1], s2s_sem.at[i - 1], s2r_sem.at[i - 1], (at(i, 0), z))

    def group_send(i):
        for j in (1, 3, 2):
            k = i * 4 + j
            sib_copy(k).wait_recv()
            block_code(s1, (j - 1) * 4 + i, acc_own[k] + sib[k])
            go(first_copy(i, j))

    group_for_sibling(1)
    group_for_sibling(3)
    group_own(1)
    group_send(1)
    group_for_sibling(2)
    group_own(3)
    group_send(3)
    group_for_sibling(0)
    group_own(2)
    group_send(2)
    group_own(0)
    group_send(0)
    for i in (1, 3, 2, 0):
        k = i * 4
        sib_copy(k).wait_recv()
        value = acc_own[k] + sib[k]
        for j in (1, 3, 2):
            first_copy(i, j).wait_recv()
            value = value + block_decode(r1, (j - 1) * 4 + i)
        if i:
            block_code(s2, i - 1, value)
            go(second_copy(i))
    for i in (1, 3, 2):
        second_copy(i).wait_recv()
        value = value + block_decode(r2, i - 1)
    own = value.astype(BF16)
    hg[7] = own
    hg_out[...] = own

    def g_place(direction, step):
        return 7 if step < 0 else min(step * 2 + direction, 6)

    def g_copy(direction, step, half):
        k = unit_index(direction, step, half)
        rows = pl.ds(half * 64, 64)
        return remote(
            hg.at[g_place(direction, step - 1), rows],
            hg.at[g_place(direction, step), rows],
            gs_sem.at[k],
            gr_sem.at[k],
            (right, left)[direction],
        )

    def unit_part(place, chunk):
        cols = dw[:, pl.ds(pl.multiple_of(chunk * FEAT, FEAT), FEAT)]
        return lax.dot_general(hg[place], cols, (((1,), (1,)), ((), ())), preferred_element_type=F32)

    for half in (0, 1):
        for direction in (0, 1):
            go(g_copy(direction, 0, half))
    dw_copy.wait()
    unit[...] = unit_part(7, z)
    for step in (1, 2, 3):
        for half in (0, 1):
            for direction in (0, 1):
                h = half if direction == 0 else 1 - half
                g_copy(direction, step - 1, h).wait_recv()
                if step < 3 or h == direction:
                    go(g_copy(direction, step, h))
        for direction in (0, 1):
            unit[...] += unit_part(g_place(direction, step - 1), away(1 - direction, step))
    for direction in (0, 1):
        g_copy(direction, 3, direction).wait_recv()
    unit[...] += unit_part(6, away(0, 4))

    for k in range(HU // TILE):
        part = slice(k * TILE, (k + 1) * TILE)
        grad = unit[:, part]
        g = gate[:, part].astype(F32)
        u = up[:, part].astype(F32)
        sig = 1.0 / (1.0 + jnp.exp(-g))
        ug_out[:, part] = (grad * g * sig).astype(BF16)
        gg_out[:, part] = (grad * u * sig * (1.0 + g * (1.0 - sig))).astype(BF16)

    for copy in sends:
        copy.wait_send()


def on_device(hidden, head_weight, lse, targets, loss_weight, block_tiles, block_counts, gate_pre, up_pre, down_weight):
    vmem = pl.BlockSpec(memory_space=pltpu.VMEM)
    hbm = pl.BlockSpec(memory_space=pl.ANY)
    dma = pltpu.SemaphoreType.DMA
    return pl.pallas_call(
        body,
        out_shape=(
            jax.ShapeDtypeStruct((TILE, FEAT), BF16),
            jax.ShapeDtypeStruct((TILE, HU), BF16),
            jax.ShapeDtypeStruct((TILE, HU), BF16),
        ),
        in_specs=[hbm, hbm, vmem, vmem, vmem, hbm, hbm, vmem, vmem, hbm],
        out_specs=(vmem, vmem, vmem),
        scratch_shapes=[
            pltpu.VMEM((BLOCKS, TILE, FEAT), BF16),
            pltpu.VMEM((VT, TILE, FEAT), BF16),
            pltpu.VMEM((HU, Z * FEAT), BF16),
            pltpu.VMEM((SLOTS, TILE, TILE), F32),
            pltpu.VMEM((SLOTS + 1, TILE, TILE), BF16),
            pltpu.VMEM((16, TILE, FEAT), F32),
            pltpu.VMEM((16, TILE, FEAT), F32),
            pltpu.VMEM((16, TILE, FEAT), F32),
            pltpu.VMEM((16, UNIT, TILE), I16),
            pltpu.VMEM((16, UNIT, TILE), I16),
            pltpu.VMEM((12, TILE + 16, FEAT), I16),
            pltpu.VMEM((12, TILE + 16, FEAT), I16),
            pltpu.VMEM((3, TILE + 16, FEAT), I16),
            pltpu.VMEM((3, TILE + 16, FEAT), I16),
            pltpu.VMEM((Z, TILE, FEAT), BF16),
            pltpu.VMEM((TILE, HU), F32),
            pltpu.VMEM((BLOCKS, 8, TILE), F32),
            pltpu.VMEM((BLOCKS, 8, TILE), F32),
            pltpu.SMEM((BLOCKS, 1, MAXT), I32),
            pltpu.SMEM((BLOCKS, 1), I32),
            pltpu.SMEM((BLOCKS + 1,), I32),
            pltpu.SMEM((SLOTS,), I32),
            pltpu.SMEM((SLOTS,), I32),
            dma((5,)),
            dma((31,)),
            dma((32,)),
            dma((16,)),
            dma((16,)),
            dma((16,)),
            dma((16,)),
            dma((16,)),
            dma((16,)),
            dma((12,)),
            dma((12,)),
            dma((3,)),
            dma((3,)),
            dma((16,)),
            dma((16,)),
        ],
        compiler_params=pltpu.CompilerParams(
            collective_id=0, has_side_effects=True, vmem_limit_bytes=60 * 2**20
        ),
        cost_estimate=pl.CostEstimate(flops=4 * 10**9, bytes_accessed=13 * 10**6, transcendentals=10**6),
    )(
        hidden,
        head_weight.reshape(VT, TILE, FEAT),
        lse.reshape(BLOCKS, TILE),
        targets.reshape(BLOCKS, TILE),
        loss_weight.reshape(BLOCKS, TILE),
        block_tiles,
        block_counts,
        gate_pre,
        up_pre,
        down_weight,
    )


def solution(mesh):
    in_specs = (
        P("wide", "narrow"),
        P("wide", "narrow"),
        P(),
        P(),
        P(),
        P(None, "wide", None),
        P(None, "wide"),
        P("wide", "narrow"),
        P("wide", "narrow"),
        P("narrow", None),
    )
    out_specs = (P("wide", "narrow"), P("wide", "narrow"), P("wide", "narrow"))
    return jax.shard_map(on_device, mesh=mesh, in_specs=in_specs, out_specs=out_specs, check_vma=False)
```

```python
import jax
import jax.numpy as jnp
from jax import lax
from jax.experimental import pallas as pl
from jax.experimental.pallas import tpu as pltpu
from jax.sharding import PartitionSpec as P

MESH = pl.DeviceIdType.MESH
F32 = jnp.float32
BF16 = jnp.bfloat16
I16 = jnp.int16
I32 = jnp.int32
TILE = 128
SLOTS = 64
BLOCKS = 32
MAXT = 4
FEAT = 512
HU = 896
VT = 32
Z = 8
HALF = 4
UNIT = HALF * TILE + 16


def scale_exponent(top):
    return jnp.clip(jnp.ceil(jnp.log2(top)), -100.0, 127.0)


def code(value, exponent):
    return jnp.round(value * jnp.exp2(14.875 - exponent)).astype(I32).astype(I16)


def factor_of(exponent16):
    return jnp.exp2(exponent16.astype(I32).astype(F32) - 14.875)


def to_f32(coded):
    return coded.astype(I32).astype(F32)


def body(
    hidden,
    weight,
    lse,
    targets,
    scale,
    tiles_in,
    counts_in,
    gate,
    up,
    down,
    hg_out,
    gg_out,
    ug_out,
    hid,
    w,
    dw,
    lp,
    probs,
    acc_own,
    acc_sib,
    sib,
    zs,
    zr,
    s1,
    r1,
    s2,
    r2,
    hg,
    unit,
    up_factor,
    gate_factor,
    lse_rows,
    scale_rows,
    tiles,
    counts,
    pos,
    slot_block,
    slot_tile,
    local_sem,
    hs_sem,
    hr_sem,
    zs_sem,
    zr_sem,
    ps_sem,
    pr_sem,
    bs_sem,
    br_sem,
    s1s_sem,
    s1r_sem,
    s2s_sem,
    s2r_sem,
    gs_sem,
    gr_sem,
):
    me = lax.axis_index("wide")
    z = lax.axis_index("narrow")
    x = me // 8
    y = (me // 2) % 4
    c = me % 2

    def placed(i, j, core):
        xi = i * (1 - core) + j * core
        yi = j * (1 - core) + i * core
        return ((x + xi) % 4) * 8 + ((y + yi) % 4) * 2 + core

    def at(i, j):
        return placed(i, j, c)

    sibling = (x * 8 + y * 2 + 1 - c, z)
    right = (me, (z + 1) % Z)
    left = (me, (z + Z - 1) % Z)

    def remote(src, dst, send, recv, device):
        return pltpu.make_async_remote_copy(
            src_ref=src, dst_ref=dst, send_sem=send, recv_sem=recv, device_id=device, device_id_type=MESH
        )

    own_copy = pltpu.make_async_copy(hidden, hid.at[me], local_sem.at[0])
    own_copy.start()
    w_copy = pltpu.make_async_copy(weight, w, local_sem.at[1])
    w_copy.start()
    dw_copy = pltpu.make_async_copy(down, dw, local_sem.at[2])
    dw_copy.start()
    tiles_copy = pltpu.make_async_copy(tiles_in, tiles, local_sem.at[3])
    tiles_copy.start()
    counts_copy = pltpu.make_async_copy(counts_in, counts, local_sem.at[4])
    counts_copy.start()

    barrier = pltpu.get_barrier_semaphore()
    peers = [sibling, right, left]
    peers += [(at(i, 0), z) for i in (1, 2, 3)] + [(at(0, j), z) for j in (1, 2, 3)]
    for peer in peers:
        pl.semaphore_signal(barrier, inc=1, device_id=peer, device_id_type=MESH)
    pl.semaphore_wait(barrier, len(peers))

    sends = []

    def go(copy):
        copy.start()
        sends.append(copy)

    def block_send(src, b, k, device):
        go(remote(src, hid.at[b], hs_sem.at[k], hr_sem.at[b], device))

    def block_wait(b):
        remote(hid.at[b], hid.at[b], hs_sem.at[0], hr_sem.at[b], sibling).wait_recv()

    for i in (1, 3, 2):
        block_send(hidden, me, i - 1, (at(i, 0), z))
    for j in (1, 3, 2):
        block_send(hidden, me, 2 + j, (at(0, j), z))
    block_send(hidden, me, 15, sibling)

    def prefix(b, run):
        pos[b] = run
        return run + counts[0, b]

    def fill(s, carry):
        before = jnp.int32(0)
        for b in range(BLOCKS):
            before = before + jnp.clip(s + 1 - pos[b + 1], 0, 1)
        b = jnp.minimum(before, BLOCKS - 1)
        j = jnp.clip(s - pos[b], 0, MAXT - 1)
        slot_block[s] = b
        slot_tile[s] = jnp.clip(tiles[j, b], 0, VT - 1)
        return carry

    lane = lax.broadcasted_iota(I32, (TILE, TILE), 1)
    first = me * (VT * TILE)

    def target_block(acc, k, b):
        ids = jnp.broadcast_to(targets[pl.ds(b, 1), :] - first, (TILE, TILE)).astype(F32).T.astype(I32)
        total = jnp.zeros((TILE, FEAT), F32)
        for v in range(0, VT, 4):
            hot = jnp.concatenate(
                [jnp.where(ids == lane + (v + u) * TILE, 1.0, 0.0).astype(BF16) for u in range(4)], axis=1
            )
            total = total + jnp.dot(hot, w[v : v + 4].reshape(4 * TILE, FEAT), preferred_element_type=F32)
        weights = jnp.broadcast_to(scale[pl.ds(b, 1), :], (TILE, TILE)).T
        for n in range(FEAT // TILE):
            part = slice(n * TILE, (n + 1) * TILE)
            acc[k, :, part] = -weights * total[:, part]

    def target_blocks(lo, hi):
        def pair(k, carry):
            target_block(acc_sib, k, placed(k // 4, k % 4, 1 - c))
            target_block(acc_own, k, placed(k // 4, k % 4, c))
            return carry

        lax.fori_loop(lo // 2, hi // 2, pair, 0)

    for i in (1, 3, 2):
        b = at(i, 0)
        block_wait(b)
        for j in (1, 3, 2):
            block_send(hid.at[b], b, 2 + i * 3 + j, (at(0, j), z))
        block_send(hid.at[b], b, 15 + i, sibling)
    tiles_copy.wait()
    counts_copy.wait()
    pos[BLOCKS] = lax.fori_loop(0, BLOCKS, prefix, jnp.int32(0))
    lax.fori_loop(0, SLOTS, fill, 0)
    for b in range(BLOCKS):
        lse_rows[b] = jnp.broadcast_to(lse[b : b + 1, :], (8, TILE))
        scale_rows[b] = jnp.broadcast_to(scale[b : b + 1, :], (8, TILE))
    probs[SLOTS] = jnp.zeros((TILE, TILE), BF16)
    w_copy.wait()
    target_blocks(0, 6)
    for j in (1, 3, 2):
        for i in (0, 1, 3, 2):
            b = at(i, j)
            block_wait(b)
            block_send(hid.at[b], b, 15 + j * 4 + i, sibling)
    own_copy.wait()
    for k in range(16):
        block_wait(2 * k + 1 - c)

    def logits(chunk):
        def slot(i, carry):
            s = chunk * 8 + i
            rows = hid[slot_block[s]]
            entries = w[slot_tile[s]]
            lp[s] = lax.dot_general(entries, rows, (((1,), (1,)), ((), ())), preferred_element_type=F32)
            return carry

        lax.fori_loop(0, 8, slot, 0, unroll=4)

    row16 = lax.broadcasted_iota(I32, (16, TILE), 0) // 4

    def unit_code(k, chunk, half, arrived):
        base = chunk * 8 + half * HALF
        if arrived is not None:
            factors = factor_of(zr[arrived, HALF * TILE : UNIT, :])

        def slot(i, exps):
            value = lp[base + i]
            if arrived is not None:
                factor = jnp.max(jnp.where(row16 == i, factors, 0.0), axis=0, keepdims=True)
                value = value + to_f32(zr[arrived, pl.ds(pl.multiple_of(i * TILE, TILE), TILE), :]) * factor
            e = scale_exponent(jnp.max(jnp.abs(value), axis=0, keepdims=True))
            zs[k, pl.ds(pl.multiple_of(i * TILE, TILE), TILE), :] = code(value, e)
            return jnp.where(row16 == i, e, exps)

        exps = lax.fori_loop(0, HALF, slot, jnp.zeros((16, TILE), F32), unroll=2)
        zs[k, HALF * TILE : UNIT, :] = exps.astype(I32).astype(I16)

    def unit_index(direction, step, half):
        return direction * 8 + step * 2 + half

    def unit_send(direction, step, half):
        k = unit_index(direction, step, half)
        go(remote(zs.at[k], zr.at[k], zs_sem.at[k], zr_sem.at[k], (right, left)[direction]))

    def unit_wait(direction, step, half):
        k = unit_index(direction, step, half)
        remote(zs.at[k], zr.at[k], zs_sem.at[k], zr_sem.at[k], right).wait_recv()
        return k

    def away(direction, distance):
        return (z + (distance if direction == 0 else Z - distance)) % Z

    def gate_factors():
        for k in range(HU // TILE):
            part = slice(k * TILE, (k + 1) * TILE)
            g = gate[:, part].astype(F32)
            sig = 1.0 / (1.0 + jnp.exp(-g))
            up_factor[:, part] = g * sig
            gate_factor[:, part] = up[:, part].astype(F32) * sig * (1.0 + g * (1.0 - sig))

    logits(away(0, 4))
    for direction in (0, 1):
        unit_code(unit_index(direction, 0, direction), away(0, 4), direction, None)
        unit_send(direction, 0, direction)
    for direction in (0, 1):
        logits(away(direction, 3))
        half = 1 - direction
        unit_code(unit_index(direction, 1, half), away(direction, 3), half, None)
        unit_send(direction, 1, half)
    logits(away(0, 2))
    logits(away(1, 2))
    for step in (1, 2, 3):
        for half in (0, 1):
            for direction in (0, 1):
                if step == 1 and half != direction:
                    continue
                k = unit_wait(direction, step - 1, half)
                unit_code(unit_index(direction, step, half), away(direction, 4 - step), half, k)
                unit_send(direction, step, half)
        if step == 1:
            logits(away(0, 1))
            logits(away(1, 1))
            logits(z)
        target_blocks(4 + step * 2, 6 + step * 2)
        if step == 2:
            gate_factors()

    def part_refs(t, chunk, half):
        return probs.at[pl.ds(chunk * 8 + half * HALF, HALF)]

    def p_send(direction, step, half):
        k = unit_index(direction, step, half)
        part = part_refs(step, away(1 - direction, step), half)
        go(remote(part, part, ps_sem.at[k], pr_sem.at[k], (right, left)[direction]))

    def p_wait(direction, step, half):
        k = unit_index(direction, step, half)
        part = part_refs(step, away(1 - direction, step + 1), half)
        remote(part, part, ps_sem.at[k], pr_sem.at[k], right).wait_recv()

    for half in (0, 1):
        ka = unit_wait(0, 3, half)
        kb = unit_wait(1, 3, half)
        fa = factor_of(zr[ka, HALF * TILE : UNIT, :])
        fb = factor_of(zr[kb, HALF * TILE : UNIT, :])

        def prob_slot(i, carry, ka=ka, kb=kb, fa=fa, fb=fb, half=half):
            s = z * 8 + half * HALF + i
            part = pl.ds(pl.multiple_of(i * TILE, TILE), TILE)
            factor_a = jnp.max(jnp.where(row16 == i, fa, 0.0), axis=0, keepdims=True)
            factor_b = jnp.max(jnp.where(row16 == i, fb, 0.0), axis=0, keepdims=True)
            value = lp[s] + to_f32(zr[ka, part, :]) * factor_a + to_f32(zr[kb, part, :]) * factor_b
            b = slot_block[s]
            value = jnp.exp(value - lse_rows[b][0:1, :]) * scale_rows[b][0:1, :]
            probs[s] = value.T.astype(BF16)
            return carry

        lax.fori_loop(0, HALF, prob_slot, 0, unroll=2)
        for direction in (0, 1):
            p_send(direction, 0, half)
    target_blocks(12, 16)
    for step in (1, 2, 3):
        for half in (0, 1):
            for direction in (0, 1):
                p_wait(direction, step - 1, half)
                if step < 3 or half == direction:
                    p_send(direction, step, half)
        target_blocks(12 + step * 4, 16 + step * 4)
    target_blocks(28, 32)
    for direction in (0, 1):
        p_wait(direction, 3, direction)

    def contribution(acc, k, b):
        taken, entries = [], []
        for j in range(MAXT):
            live = jnp.clip(counts[0, b] - j, 0, 1)
            taken.append(probs[jnp.clip(live * (pos[b] + j) + (1 - live) * SLOTS, 0, SLOTS)])
            entries.append(w[jnp.clip(tiles[j, b], 0, VT - 1)])
        acc[k] = acc[k] + jnp.dot(
            jnp.concatenate(taken, axis=1), jnp.concatenate(entries, axis=0), preferred_element_type=F32
        )

    def sib_copy(k):
        return remote(acc_sib.at[k], sib.at[k], bs_sem.at[k], br_sem.at[k], sibling)

    def group_for_sibling(i):
        def one(k, carry):
            contribution(acc_sib, k, placed(k // 4, k % 4, 1 - c))
            return carry

        lax.fori_loop(i * 4, i * 4 + 4, one, 0, unroll=2)
        for j in range(4):
            go(sib_copy(i * 4 + j))

    def group_own(i):
        def one(k, carry):
            contribution(acc_own, k, placed(k // 4, k % 4, c))
            return carry

        lax.fori_loop(i * 4, i * 4 + 4, one, 0, unroll=2)

    def block_code(dst, k, value):
        e = scale_exponent(jnp.max(jnp.abs(value), axis=0, keepdims=True))
        dst[k, 0:TILE, :] = code(value, e)
        dst[k, TILE : TILE + 16, :] = jnp.broadcast_to(e, (16, FEAT)).astype(I32).astype(I16)

    def block_decode(src, k):
        factor = factor_of(src[k, TILE : TILE + 16, :])[0:1, :]
        return to_f32(src[k, 0:TILE, :]) * factor

    def first_copy(i, j):
        k = (j - 1) * 4 + i
        return remote(s1.at[k], r1.at[k], s1s_sem.at[k], s1r_sem.at[k], (at(0, j), z))

    def second_copy(i):
        return remote(s2.at[i - 1], r2.at[i - 1], s2s_sem.at[i - 1], s2r_sem.at[i - 1], (at(i, 0), z))

    def group_send(i):
        for j in (1, 3, 2):
            k = i * 4 + j
            sib_copy(k).wait_recv()
            block_code(s1, (j - 1) * 4 + i, acc_own[k] + sib[k])
            go(first_copy(i, j))

    group_for_sibling(1)
    group_for_sibling(3)
    group_own(1)
    group_send(1)
    group_for_sibling(2)
    group_own(3)
    group_send(3)
    group_for_sibling(0)
    group_own(2)
    group_send(2)
    group_own(0)
    group_send(0)
    for i in (1, 3, 2, 0):
        k = i * 4
        sib_copy(k).wait_recv()
        value = acc_own[k] + sib[k]
        for j in (1, 3, 2):
            first_copy(i, j).wait_recv()
            value = value + block_decode(r1, (j - 1) * 4 + i)
        if i:
            block_code(s2, i - 1, value)
            go(second_copy(i))
    for i in (1, 3, 2):
        second_copy(i).wait_recv()
        value = value + block_decode(r2, i - 1)
    own = value.astype(BF16)
    hg[7] = own
    hg_out[...] = own

    def g_place(direction, step):
        return 7 if step < 0 else min(step * 2 + direction, 6)

    def g_copy(direction, step, half):
        k = unit_index(direction, step, half)
        rows = pl.ds(half * 64, 64)
        return remote(
            hg.at[g_place(direction, step - 1), rows],
            hg.at[g_place(direction, step), rows],
            gs_sem.at[k],
            gr_sem.at[k],
            (right, left)[direction],
        )

    def unit_part(place, chunk):
        cols = dw[:, pl.ds(pl.multiple_of(chunk * FEAT, FEAT), FEAT)]
        return lax.dot_general(hg[place], cols, (((1,), (1,)), ((), ())), preferred_element_type=F32)

    for half in (0, 1):
        for direction in (0, 1):
            go(g_copy(direction, 0, half))
    dw_copy.wait()
    unit[...] = unit_part(7, z)
    for step in (1, 2, 3):
        for half in (0, 1):
            for direction in (0, 1):
                g_copy(direction, step - 1, half).wait_recv()
                if step < 3 or half == direction:
                    go(g_copy(direction, step, half))
        for direction in (0, 1):
            unit[...] += unit_part(g_place(direction, step - 1), away(1 - direction, step))
    for direction in (0, 1):
        g_copy(direction, 3, direction).wait_recv()
    unit[...] += unit_part(6, away(0, 4))

    for k in range(HU // TILE):
        part = slice(k * TILE, (k + 1) * TILE)
        grad = unit[:, part]
        ug_out[:, part] = (grad * up_factor[:, part]).astype(BF16)
        gg_out[:, part] = (grad * gate_factor[:, part]).astype(BF16)

    for copy in sends:
        copy.wait_send()


def on_device(hidden, head_weight, lse, targets, loss_weight, block_tiles, block_counts, gate_pre, up_pre, down_weight):
    vmem = pl.BlockSpec(memory_space=pltpu.VMEM)
    hbm = pl.BlockSpec(memory_space=pl.ANY)
    dma = pltpu.SemaphoreType.DMA
    return pl.pallas_call(
        body,
        out_shape=(
            jax.ShapeDtypeStruct((TILE, FEAT), BF16),
            jax.ShapeDtypeStruct((TILE, HU), BF16),
            jax.ShapeDtypeStruct((TILE, HU), BF16),
        ),
        in_specs=[hbm, hbm, vmem, vmem, vmem, hbm, hbm, vmem, vmem, hbm],
        out_specs=(vmem, vmem, vmem),
        scratch_shapes=[
            pltpu.VMEM((BLOCKS, TILE, FEAT), BF16),
            pltpu.VMEM((VT, TILE, FEAT), BF16),
            pltpu.VMEM((HU, Z * FEAT), BF16),
            pltpu.VMEM((SLOTS, TILE, TILE), F32),
            pltpu.VMEM((SLOTS + 1, TILE, TILE), BF16),
            pltpu.VMEM((16, TILE, FEAT), F32),
            pltpu.VMEM((16, TILE, FEAT), F32),
            pltpu.VMEM((16, TILE, FEAT), F32),
            pltpu.VMEM((16, UNIT, TILE), I16),
            pltpu.VMEM((16, UNIT, TILE), I16),
            pltpu.VMEM((12, TILE + 16, FEAT), I16),
            pltpu.VMEM((12, TILE + 16, FEAT), I16),
            pltpu.VMEM((3, TILE + 16, FEAT), I16),
            pltpu.VMEM((3, TILE + 16, FEAT), I16),
            pltpu.VMEM((Z, TILE, FEAT), BF16),
            pltpu.VMEM((TILE, HU), F32),
            pltpu.VMEM((TILE, HU), F32),
            pltpu.VMEM((TILE, HU), F32),
            pltpu.VMEM((BLOCKS, 8, TILE), F32),
            pltpu.VMEM((BLOCKS, 8, TILE), F32),
            pltpu.SMEM((MAXT, BLOCKS), I32),
            pltpu.SMEM((1, BLOCKS), I32),
            pltpu.SMEM((BLOCKS + 1,), I32),
            pltpu.SMEM((SLOTS,), I32),
            pltpu.SMEM((SLOTS,), I32),
            dma((5,)),
            dma((31,)),
            dma((32,)),
            dma((16,)),
            dma((16,)),
            dma((16,)),
            dma((16,)),
            dma((16,)),
            dma((16,)),
            dma((12,)),
            dma((12,)),
            dma((3,)),
            dma((3,)),
            dma((16,)),
            dma((16,)),
        ],
        compiler_params=pltpu.CompilerParams(
            collective_id=0, has_side_effects=True, vmem_limit_bytes=60 * 2**20
        ),
        cost_estimate=pl.CostEstimate(flops=4 * 10**9, bytes_accessed=13 * 10**6, transcendentals=10**6),
    )(
        hidden,
        head_weight.reshape(VT, TILE, FEAT),
        lse.reshape(BLOCKS, TILE),
        targets.reshape(BLOCKS, TILE),
        loss_weight.reshape(BLOCKS, TILE),
        block_tiles[:, 0, :].T,
        block_counts.T,
        gate_pre,
        up_pre,
        down_weight,
    )


def solution(mesh):
    in_specs = (
        P("wide", "narrow"),
        P("wide", "narrow"),
        P(),
        P(),
        P(),
        P(None, "wide", None),
        P(None, "wide"),
        P("wide", "narrow"),
        P("wide", "narrow"),
        P("narrow", None),
    )
    out_specs = (P("wide", "narrow"), P("wide", "narrow"), P("wide", "narrow"))
    return jax.shard_map(on_device, mesh=mesh, in_specs=in_specs, out_specs=out_specs, check_vma=False)
```
